256 devices in a mesh: step: 8 (over x_lo, y), ctx: 32 (over x_hi, z, core).
Axes of the slice: x: 4 (x_hi: 2, x_lo: 2; x = x_hi * 2 + x_lo), y: 4, z: 8, core: 2. Of those that a mesh axis runs over, the one named last changes fastest.
Arguments:
- latent: bfloat16 [8, 2048, 4096], P('step', 'ctx'), may hold values from -6 to 6
- span_queries: bfloat16 [8, 2048, 4096], P('step', 'ctx'), may hold values from -8 to 8
- span_keys: bfloat16 [8, 2048, 4096], P('step', 'ctx'), may hold values from -8 to 8
- span_values: bfloat16 [8, 2048, 4096], P('step', 'ctx'), may hold values from -6 to 6
- cache_keys: bfloat16 [4096, 4096], P(None, 'ctx'), may hold values from -6 to 6
- cache_values: bfloat16 [4096, 4096], P(None, 'ctx'), may hold values from -6 to 6
- time_weight: bfloat16 [256, 4096], P(None, 'ctx'), may hold values from -4 to 4
- timestep: int32 [8], replicated, may hold values from 0 to 999, as said below
- span_index: int32 [8], replicated, may hold values from 67 to 80, as said below
- prefix_spans: int32 [8], replicated, may hold values from 1 to 2, as said below
Outputs:
- advanced: bfloat16 [8, 2048, 4096], P('step', 'ctx')
The draws below stay inside these ranges and needn't reach their ends.
Inputs may be any that keep to these rules, and one draw needn't show every extreme that they name: `timestep`: timesteps fall strictly from group to group; the first group's is 999 and the last group's is 0. `span_index`: span numbers fall from group to group by 2, except at exactly one step where they fall by 1; the first group's is 80. `prefix_spans`: some group sees all 2 cached spans.
All inputs are finite; a program needn't handle non-finite values.
Results may differ from the reference program's by a relative error of at most 0.012.
Values may be sent and summed in bfloat16 or wider, within the bound.
A program may use at most 128 MiB of HBM per device.

```python
import math
import jax
import jax.numpy as jnp
from jax import lax

HEADS = 32
HEAD_DIM = 128
FREQS = 256
FRAMES = 3
CACHE_CH = 2
STEPS = 8
TOKENS = 2048
W = 4096


def draw_span_queries(key, part):
    key = jax.random.fold_in(key, 11)
    base = jnp.clip(2.0 * jax.random.normal(key, (STEPS, TOKENS, HEADS * HEAD_DIM), jnp.float32), -8.0, 8.0)
    return base.astype(jnp.bfloat16)


def draw_span_keys(key, part):
    key = jax.random.fold_in(key, 12)
    base = jnp.clip(jax.random.normal(key, (STEPS, TOKENS, HEADS * HEAD_DIM), jnp.float32), -8.0, 8.0)
    return base.astype(jnp.bfloat16)


def reverse_totals(increments):
    return jnp.flip(jnp.cumsum(jnp.flip(increments))) - increments


def draw_timestep(key, part):
    key = jax.random.fold_in(key, 21)
    increments = jax.random.randint(key, (STEPS,), 1, 999 // STEPS + 1, dtype=jnp.int32)
    levels = reverse_totals(increments)
    first_row = jnp.arange(STEPS, dtype=jnp.int32) == 0
    return jnp.where(first_row, 999, levels).astype(jnp.int32)


def draw_span_index(key, part):
    key = jax.random.fold_in(key, 22)
    single = jax.random.randint(key, (), 0, STEPS - 1, dtype=jnp.int32)
    increments = jnp.where(jnp.arange(STEPS, dtype=jnp.int32) == single, 1, 2).astype(jnp.int32)
    before = jnp.cumsum(increments) - increments
    return (64 + 2 * STEPS - before).astype(jnp.int32)


def draw_prefix_spans(key, part):
    key = jax.random.fold_in(key, 23)
    first_key, second_key = jax.random.split(key)
    counts = jax.random.randint(first_key, (STEPS,), 1, CACHE_CH + 1, dtype=jnp.int32)
    fullest = jax.random.randint(second_key, (), 0, STEPS, dtype=jnp.int32)
    return jnp.where(jnp.arange(STEPS, dtype=jnp.int32) == fullest, CACHE_CH, counts).astype(jnp.int32)


def steps_of(rng, extent, cuts, low, top_value):
    def one(axis_at, shards_of):
        draws = jax.random.uniform(jax.random.fold_in(jax.random.fold_in(rng, 6), axis_at), (shards_of,), jnp.float32, low / len(cuts), top_value / len(cuts))
        return jnp.repeat(jnp.exp(draws), extent[axis_at] // shards_of).reshape((-1,) + (1,) * (len(extent) - axis_at - 1))

    factor_of = one(*cuts[0])
    for cut in cuts[1:]:
        factor_of = factor_of * one(*cut)
    return factor_of


def scatter_about(key, shape, spread, limit, shards=(), kind=jnp.bfloat16):
    loudness = steps_of(key, shape, shards, -0.22, 0.18) if shards else 1.0
    result = jax.random.normal(key, shape, jnp.float32) * spread * loudness
    return jnp.minimum(jnp.maximum(result, -limit), limit).astype(kind)


def setup_inputs(seed: int = 0) -> dict:
    streams_of = jax.random.split(jax.random.key(seed), 11)
    return {
        "latent": scatter_about(streams_of[0], (STEPS, TOKENS, W), 1.0, 6.0, ((0, 8), (1, 32))),
        "span_queries": draw_span_queries(jax.random.fold_in(streams_of[10], 71), 0),
        "span_keys": draw_span_keys(jax.random.fold_in(streams_of[10], 71), 0),
        "span_values": scatter_about(streams_of[3], (STEPS, TOKENS, W), 1.0, 6.0, ((0, 8), (1, 32))),
        "cache_keys": scatter_about(streams_of[4], (CACHE_CH * TOKENS, W), 1.0, 6.0, ((1, 32),)),
        "cache_values": scatter_about(streams_of[5], (CACHE_CH * TOKENS, W), 1.0, 6.0, ((1, 32),)),
        "time_weight": scatter_about(streams_of[6], (FREQS, W), 2 ** -0.5, 4.0, ((1, 32),)),
        "timestep": draw_timestep(jax.random.fold_in(streams_of[10], 71), 0),
        "span_index": draw_span_index(jax.random.fold_in(streams_of[10], 71), 0),
        "prefix_spans": draw_prefix_spans(jax.random.fold_in(streams_of[10], 71), 0),
    }


def rotary(field, positions):
    halves = HEAD_DIM // 2
    inverse = 10000.0 ** (-jnp.arange(halves, dtype=jnp.float32) / halves)
    angles = positions[:, None] * inverse[None, :]
    cosine = jnp.cos(angles)[:, None, :]
    sine = jnp.sin(angles)[:, None, :]
    shaped = field.astype(jnp.float32).reshape(field.shape[0], -1, 2, halves)
    first = shaped[:, :, 0]
    second = shaped[:, :, 1]
    turned = jnp.stack([first * cosine - second * sine, second * cosine + first * sine], axis=2)
    return turned.reshape(field.shape).astype(jnp.bfloat16)

def frame_positions(span_number, row_count):
    row_index = jnp.arange(row_count, dtype=jnp.int32)
    frames = span_number.astype(jnp.int32) * FRAMES + row_index * FRAMES // TOKENS
    return frames.astype(jnp.float32)

def time_gate(level, time_weight):
    halves = FREQS // 2
    freqs = 10000.0 ** (-jnp.arange(halves, dtype=jnp.float32) / halves)
    angles = level.astype(jnp.float32) * freqs
    embedded = jnp.concatenate([jnp.cos(angles), jnp.sin(angles)])
    return jnp.dot(embedded, time_weight.astype(jnp.float32), precision=lax.Precision.HIGHEST)

def attend_head(query_head, key_head, value_head, visible):
    scores = jnp.dot(query_head, key_head.T, preferred_element_type=jnp.float32) * (1.0 / math.sqrt(HEAD_DIM))
    scores = jnp.where(visible[None, :], scores, -jnp.inf)
    peak = lax.optimization_barrier(jnp.max(scores, axis=1, keepdims=True))
    weights = jnp.exp(scores - peak)
    totals = lax.optimization_barrier(jnp.sum(weights, axis=1, keepdims=True))
    mixed = jnp.dot(weights.astype(jnp.bfloat16), value_head, preferred_element_type=jnp.float32)
    return mixed / totals

def reference(latent, span_queries, span_keys, span_values, cache_keys, cache_values, time_weight, timestep, span_index, prefix_spans):
    final_group = STEPS - 1
    fresh_keys = rotary(span_keys[final_group], frame_positions(span_index[final_group], TOKENS))
    fresh_values = span_values[final_group]
    slot = jnp.arange((CACHE_CH + 2) * TOKENS, dtype=jnp.int32) // TOKENS
    results = []
    for section in range(STEPS):
        positions = frame_positions(span_index[section], TOKENS)
        queries = rotary(span_queries[section], positions)
        own_keys = rotary(span_keys[section], positions)
        keys_all = jnp.concatenate([cache_keys, fresh_keys, own_keys], 0)
        values_all = jnp.concatenate([cache_values, fresh_values, span_values[section]], 0)
        visible = jnp.where(slot < CACHE_CH, slot >= CACHE_CH - prefix_spans[section], jnp.where(slot == CACHE_CH, section != final_group, True))
        query_heads = queries.reshape(TOKENS, HEADS, HEAD_DIM).transpose(1, 0, 2)
        key_heads = keys_all.reshape(-1, HEADS, HEAD_DIM).transpose(1, 0, 2)
        value_heads = values_all.reshape(-1, HEADS, HEAD_DIM).transpose(1, 0, 2)
        per_head = lax.map(lambda packed: attend_head(packed[0], packed[1], packed[2], visible), (query_heads, key_heads, value_heads))
        attention = per_head.transpose(1, 0, 2).reshape(TOKENS, W)
        gated = (attention * time_gate(timestep[section], time_weight)[None, :]).astype(jnp.bfloat16)
        gated = lax.optimization_barrier(gated)
        updated = (latent[section].astype(jnp.float32) + gated.astype(jnp.float32)).astype(jnp.bfloat16)
        results.append(updated)
    return jnp.roll(jnp.stack(results), 1, axis=0)
```

```python
import functools
import math

import jax
import jax.numpy as jnp
import numpy as np
from jax import lax
from jax.experimental import pallas as pl
from jax.experimental.pallas import tpu as pltpu
from jax.sharding import PartitionSpec as P

MESH = pl.DeviceIdType.MESH
HEAD_DIM = 128
FREQS = 256
FRAMES = 3
BLOCK = 256
CHUNK = 512
FAR = 1e30

TREES = (
    ((0, 1, 2, 6), (5,), (1, 2)),
    ((7,), (0, 3, 2, 7, 6), (3,)),
    ((4, 5), (4,), (0, 6, 5, 7)),
)
PART_ROWS = (704, 640, 704)
PARTS = 4


def table():
    n = FREQS // 2
    gate = 10000.0 ** (-np.arange(n, dtype=np.float64) / n)
    half = HEAD_DIM // 2
    turn = 10000.0 ** (-np.arange(half, dtype=np.float64) / half)
    rows = np.concatenate([np.repeat(gate[:, None], 128, 1), np.repeat(np.tile(turn, 2)[None], 8, 0)])
    return rows.astype(np.float32)


def kernel(
    times_ref, spans_ref, prefix_ref, freq_ref, latent_ref, q_ref, k_ref, v_ref, ck_ref, cv_ref, tw_ref,
    moved_ref, gated_ref,
    freq, q_in, k_in, ck, cv, tw, q_out, k_out, qh, kh, vh, kc, vc, acc, peak, gate, mine,
    load_sem, q_sent, q_got, kv_sent, kv_got, c_sent, c_got, o_sent, o_got, l_sent, l_got, next_in,
):
    groups, width = lax.axis_size("step"), lax.axis_size("ctx")
    g, me = lax.axis_index("step"), lax.axis_index("ctx")
    rows = q_ref.shape[0]
    total = rows * width
    blocks = total // BLOCK
    per = BLOCK // rows
    last = groups - 1
    clean = g == last
    after, before = lax.rem(g + 1, groups), lax.rem(g + groups - 1, groups)
    gx, gy = lax.div(g, 4), lax.rem(g, 4)
    near = (
        gx * 4 + lax.rem(gy + 1, 4),
        gx * 4 + lax.rem(gy + 3, 4),
        (1 - gx) * 4 + gy,
    )
    node = (1 - gx) * 4 + lax.rem(gy + 1, 4)

    loads = [
        pltpu.make_async_copy(a, b, load_sem.at[i])
        for i, (a, b) in enumerate(
            ((q_ref, q_in), (k_ref, k_in), (freq_ref, freq), (tw_ref, tw), (ck_ref, ck), (cv_ref, cv))
        )
    ]
    for load in loads:
        load.start()

    barrier = pltpu.get_barrier_semaphore()

    def greet(i, _):
        pl.semaphore_signal(barrier, inc=1, device_id={"ctx": lax.rem(me + i, width)}, device_id_type=MESH)
        return 0

    lax.fori_loop(1, width, greet, 0)
    for other in near + (after, before):
        pl.semaphore_signal(barrier, inc=1, device_id={"step": other}, device_id_type=MESH)

    loads[2].wait()
    row = me * rows + lax.broadcasted_iota(jnp.int32, (rows, 128), 0)
    frames = spans_ref[g] * FRAMES + lax.div(row * FRAMES, total)
    angles = frames.astype(jnp.float32) * freq[128:129, :]
    cosine = jnp.cos(angles)
    lane = lax.broadcasted_iota(jnp.int32, (rows, 128), 1)
    sine = jnp.where(lane < HEAD_DIM // 2, -jnp.sin(angles), jnp.sin(angles))
    scale = math.log2(math.e) / math.sqrt(HEAD_DIM)
    loads[0].wait()
    loads[1].wait()

    def turn(h, _):
        cols = pl.ds(pl.multiple_of(h * 128, 128), 128)
        q = q_in[:, cols].astype(jnp.float32)
        k = k_in[:, cols].astype(jnp.float32)
        q_out[h] = ((q * cosine + pltpu.roll(q, 64, 1) * sine) * scale).astype(jnp.bfloat16)
        k_out[h] = (k * cosine + pltpu.roll(k, 64, 1) * sine).astype(jnp.bfloat16)
        return 0

    lax.fori_loop(0, width, turn, 0)
    pl.semaphore_wait(barrier, width - 1 + 5)
    pl.semaphore_signal(next_in, inc=1, device_id={"step": before}, device_id_type=MESH)

    my_rows = pl.ds(pl.multiple_of(me * rows, rows), rows)
    my_block = lax.div(me, per)

    def q_to(t):
        return pltpu.make_async_remote_copy(
            q_out.at[t], qh.at[my_rows], q_sent, q_got.at[my_block], device_id={"ctx": t}, device_id_type=MESH
        )

    def k_to(t):
        return pltpu.make_async_remote_copy(
            k_out.at[t], kh.at[my_rows], kv_sent.at[0], kv_got.at[0], device_id={"ctx": t}, device_id_type=MESH
        )

    def v_of(t):
        return v_ref.at[:, pl.ds(pl.multiple_of(t * 128, 128), 128)]

    def v_to(t):
        return pltpu.make_async_remote_copy(
            v_of(t), vh.at[my_rows], kv_sent.at[1], kv_got.at[1], device_id={"ctx": t}, device_id_type=MESH
        )

    def send_all(copy_to):
        def send(i, _):
            copy_to(lax.rem(me + i, width)).start()
            return 0

        lax.fori_loop(1, width, send, 0)

    @pl.when(jnp.logical_not(clean))
    def _():
        send_all(q_to)

    send_all(k_to)
    send_all(v_to)

    @pl.when(clean)
    def _():
        send_all(q_to)

    pltpu.make_async_copy(q_out.at[me], qh.at[my_rows], q_got.at[my_block]).start()
    pltpu.make_async_copy(k_out.at[me], kh.at[my_rows], kv_got.at[0]).start()
    pltpu.make_async_copy(v_of(me), vh.at[my_rows], kv_got.at[1]).start()
    latent_copy = pltpu.make_async_remote_copy(
        latent_ref, moved_ref, l_sent, l_got, device_id={"step": after}, device_id_type=MESH
    )
    latent_copy.start()

    loads[3].wait()
    turns = times_ref[g].astype(jnp.float32) * freq[0:128, :]
    gate[...] = jnp.sum(
        jnp.cos(turns) * tw[0:128, :].astype(jnp.float32) + jnp.sin(turns) * tw[128:256, :].astype(jnp.float32),
        axis=0,
        keepdims=True,
    )
    loads[4].wait()
    loads[5].wait()

    def passes(tree, way):
        return functools.reduce(jnp.logical_or, [node == n for n in TREES[tree][way]])

    def part_rows(tree, part):
        size = PART_ROWS[tree] // PARTS
        return pl.ds(sum(PART_ROWS[:tree]) + part * size, size)

    def part_copy(source, target, which, tree, part, way):
        return pltpu.make_async_remote_copy(
            source.at[part_rows(tree, part)],
            target.at[part_rows(tree, part)],
            c_sent.at[which, tree, way],
            c_got.at[which, tree, part],
            device_id={"step": near[way]},
            device_id_type=MESH,
        )

    def start_clean(source, target, which):
        for part in range(PARTS):
            for tree in range(3):
                for way in range(3):
                    if 0 in TREES[tree][way]:
                        part_copy(source, target, which, tree, part, way).start()

    def pass_clean(target, which):
        for part in range(PARTS):
            for tree in range(3):
                place = target.at[part_rows(tree, part)]
                pltpu.make_async_copy(place, place, c_got.at[which, tree, part]).wait()
                for way in range(3):
                    if any(n != 0 for n in TREES[tree][way]):

                        @pl.when(passes(tree, way))
                        def _():
                            part_copy(target, target, which, tree, part, way).start()

    def got(place, sem):
        pltpu.make_async_copy(place, place, sem).wait()

    far = (2 - prefix_ref[g]).astype(jnp.float32) * FAR
    ones = jnp.ones((CHUNK, 128), jnp.bfloat16)

    def attend(state, q, keys, values, start, stop, masked):
        for at in range(start, stop, CHUNK):
            s = lax.dot_general(
                q, keys[at : at + CHUNK, :], (((1,), (1,)), ((), ())), preferred_element_type=jnp.float32
            )
            top = jnp.max(s, axis=1, keepdims=True)
            if masked:
                top = top - far
            if state is not None:
                old, total_so_far = state
                top = jnp.maximum(old, top)
            p = jnp.exp2(s - (top + far if masked else top)).astype(jnp.bfloat16)
            mixed = jnp.dot(
                p, jnp.concatenate([values[at : at + CHUNK, :], ones], axis=1), preferred_element_type=jnp.float32
            )
            if state is not None:
                mixed = mixed + total_so_far * jnp.exp2(old - top)
            state = top, mixed
        return state

    def step(i, _):
        first = jnp.where(clean, lax.rem(i, 2) == 0, i < blocks)
        count = jnp.where(clean, lax.div(i, 2), lax.rem(i, blocks))
        block = lax.rem(my_block + 2 * blocks - 1 - count, blocks)
        here = pl.ds(pl.multiple_of(block * BLOCK, BLOCK), BLOCK)

        @pl.when(jnp.logical_and(jnp.logical_not(clean), i == blocks // 2))
        def _():
            pass_clean(kc, 0)

        @pl.when(jnp.logical_and(jnp.logical_not(clean), i == blocks))
        def _():
            pass_clean(vc, 1)
            got(kh, kv_got.at[0])
            got(vh, kv_got.at[1])

        @pl.when(i == jnp.where(clean, 1, blocks))
        def _():
            pl.semaphore_wait(next_in, 1)

        @pl.when(first)
        def _():
            got(qh.at[here], q_got.at[block])
            q = qh[here, :]
            state = attend(None, q, ck, cv, total, 2 * total, False)
            top, mixed = attend(state, q, ck, cv, 0, total, True)
            acc[here, :] = mixed
            peak[here, :] = jnp.broadcast_to(top, (BLOCK, 128))

        @pl.when(jnp.logical_not(first))
        def _():
            q = qh[here, :]

            @pl.when(jnp.logical_not(clean))
            def _():
                top, mixed = attend((peak[here, 0:1], acc[here, :]), q, kc, vc, 0, total, False)
                acc[here, :] = mixed
                peak[here, :] = jnp.broadcast_to(top, (BLOCK, 128))

            _, mixed = attend((peak[here, 0:1], acc[here, :]), q, kh, vh, 0, total, False)
            mine[here, :] = (mixed[:, :128] / mixed[:, 128:] * gate[...]).astype(jnp.bfloat16)
            for s in range(per):
                owner = block * per + s
                pltpu.make_async_remote_copy(
                    mine.at[pl.ds(pl.multiple_of(owner * rows, rows), rows)],
                    gated_ref.at[:, pl.ds(pl.multiple_of(me * 128, 128), 128)],
                    o_sent,
                    o_got,
                    device_id={"step": after, "ctx": owner},
                    device_id_type=MESH,
                ).start()

        return 0

    @pl.when(clean)
    def _():
        got(kh, kv_got.at[0])
        start_clean(kh, kc, 0)
        got(vh, kv_got.at[1])
        start_clean(vh, vc, 1)

    lax.fori_loop(0, 2 * blocks, step, 0)

    sent = qh.at[pl.ds(0, total - rows)]
    got(sent, q_sent)
    got(sent, kv_sent.at[0])
    got(sent, kv_sent.at[1])
    for which in range(2):
        for tree in range(3):
            place = kc.at[pl.ds(0, PART_ROWS[tree])]
            for way in range(3):

                @pl.when(passes(tree, way))
                def _():
                    got(place, c_sent.at[which, tree, way])

    latent_copy.wait()
    got(mine, o_sent)
    got(gated_ref, o_got)


def body(latent, q, k, v, cache_keys, cache_values, time_weight, timestep, span_index, prefix_spans):
    rows, width = q.shape[1:]
    total = cache_keys.shape[0] // 2
    half = jnp.bfloat16
    smem = pl.BlockSpec(memory_space=pltpu.SMEM)
    hbm = pl.BlockSpec(memory_space=pl.ANY)
    dma = pltpu.SemaphoreType.DMA
    freqs = table()
    moved, gated = pl.pallas_call(
        kernel,
        out_shape=[jax.ShapeDtypeStruct((rows, width), half)] * 2,
        in_specs=[smem] * 3 + [hbm] * 8,
        out_specs=[hbm] * 2,
        scratch_shapes=[
            pltpu.VMEM(freqs.shape, jnp.float32),
            pltpu.VMEM((rows, width), half),
            pltpu.VMEM((rows, width), half),
            pltpu.VMEM((2 * total, 128), half),
            pltpu.VMEM((2 * total, 128), half),
            pltpu.VMEM((FREQS, 128), half),
            pltpu.VMEM((width // 128, rows, 128), half),
            pltpu.VMEM((width // 128, rows, 128), half),
            pltpu.VMEM((total, 128), half),
            pltpu.VMEM((total, 128), half),
            pltpu.VMEM((total, 128), half),
            pltpu.VMEM((total, 128), half),
            pltpu.VMEM((total, 128), half),
            pltpu.VMEM((total, 256), jnp.float32),
            pltpu.VMEM((total, 128), jnp.float32),
            pltpu.VMEM((1, 128), jnp.float32),
            pltpu.VMEM((total, 128), half),
            dma((6,)),
            dma,
            dma((total // BLOCK,)),
            dma((2,)),
            dma((2,)),
            dma((2, 3, 3)),
            dma((2, 3, PARTS)),
            dma,
            dma,
            dma,
            dma,
            pltpu.SemaphoreType.REGULAR,
        ],
        compiler_params=pltpu.CompilerParams(
            collective_id=0, has_side_effects=True, vmem_limit_bytes=56 * 1024 * 1024
        ),
    )(timestep, span_index, prefix_spans, jnp.asarray(freqs), latent[0], q[0], k[0], v[0], cache_keys, cache_values, time_weight)
    advanced = (moved.astype(jnp.float32) + gated.astype(jnp.float32)).astype(half)
    return advanced[None]


def solution(mesh):
    spans = P("step", "ctx", None)
    heads = P(None, "ctx")
    return jax.shard_map(
        body,
        mesh=mesh,
        in_specs=(spans,) * 4 + (heads,) * 3 + (P(),) * 3,
        out_specs=spans,
        check_vma=False,
    )
```

```python
import functools
import math

import jax
import jax.numpy as jnp
import numpy as np
from jax import lax
from jax.experimental import pallas as pl
from jax.experimental.pallas import tpu as pltpu
from jax.sharding import PartitionSpec as P

MESH = pl.DeviceIdType.MESH
HEAD_DIM = 128
FREQS = 256
FRAMES = 3
BLOCK = 256
CHUNK = 512
FAR = 1e30


EARLY = 24
PASS_KEYS = 2
PASS_VALUES = 8


def table():
    n = FREQS // 2
    gate = 10000.0 ** (-np.arange(n, dtype=np.float64) / n)
    half = HEAD_DIM // 2
    turn = 10000.0 ** (-np.arange(half, dtype=np.float64) / half)
    rows = np.concatenate([np.repeat(gate[:, None], 128, 1), np.repeat(np.tile(turn, 2)[None], 8, 0)])
    return rows.astype(np.float32)


def kernel(
    times_ref, spans_ref, prefix_ref, freq_ref, latent_ref, q_ref, k_ref, v_ref, ck_ref, cv_ref, tw_ref,
    moved_ref, gated_ref,
    freq, q_in, k_in, ck, cv, tw, q_out, k_out, qh, kh, vh, kc, vc, acc, peak, gate, mine,
    load_sem, q_sent, k_sent, v_sent, q_got, kv_got, hold_got, first_sent, c_sent, c_got, o_sent, o_got, l_sent, l_got, next_in, all_in,
):
    groups, width = lax.axis_size("step"), lax.axis_size("ctx")
    g, me = lax.axis_index("step"), lax.axis_index("ctx")
    rows = q_ref.shape[0]
    total = rows * width
    blocks = total // BLOCK
    per = BLOCK // rows
    last = groups - 1
    clean = g == last
    after, before = lax.rem(g + 1, groups), lax.rem(g + groups - 1, groups)
    held = lax.rem(g + groups * width - me, groups)

    loads = [
        pltpu.make_async_copy(a, b, load_sem.at[i])
        for i, (a, b) in enumerate(
            ((q_ref, q_in), (k_ref, k_in), (freq_ref, freq), (tw_ref, tw), (ck_ref, ck), (cv_ref, cv))
        )
    ]
    for load in loads:
        load.start()

    barrier = pltpu.get_barrier_semaphore()

    def greet(i, _):
        pl.semaphore_signal(barrier, inc=1, device_id={"ctx": lax.rem(me + i, width)}, device_id_type=MESH)
        return 0

    lax.fori_loop(1, width, greet, 0)

    def greet_step(i, _):
        pl.semaphore_signal(barrier, inc=1, device_id={"step": lax.rem(g + i, groups)}, device_id_type=MESH)
        return 0

    lax.fori_loop(1, groups, greet_step, 0)

    loads[2].wait()
    row = me * rows + lax.broadcasted_iota(jnp.int32, (rows, 128), 0)
    frames = spans_ref[g] * FRAMES + lax.div(row * FRAMES, total)
    angles = frames.astype(jnp.float32) * freq[128:129, :]
    cosine = jnp.cos(angles)
    lane = lax.broadcasted_iota(jnp.int32, (rows, 128), 1)
    sine = jnp.where(lane < HEAD_DIM // 2, -jnp.sin(angles), jnp.sin(angles))
    scale = math.log2(math.e) / math.sqrt(HEAD_DIM)
    loads[0].wait()
    loads[1].wait()

    def turn(h, _):
        cols = pl.ds(pl.multiple_of(h * 128, 128), 128)
        q = q_in[:, cols].astype(jnp.float32)
        k = k_in[:, cols].astype(jnp.float32)
        q_out[h] = ((q * cosine + pltpu.roll(q, 64, 1) * sine) * scale).astype(jnp.bfloat16)
        k_out[h] = (k * cosine + pltpu.roll(k, 64, 1) * sine).astype(jnp.bfloat16)
        return 0

    lax.fori_loop(0, width, turn, 0)
    pl.semaphore_wait(barrier, width + groups - 2)
    pl.semaphore_signal(next_in, inc=1, device_id={"step": before}, device_id_type=MESH)

    @pl.when(jnp.logical_not(clean))
    def _():
        pl.semaphore_signal(all_in, inc=1, device_id={"step": last}, device_id_type=MESH)

    my_rows = pl.ds(pl.multiple_of(me * rows, rows), rows)
    my_block = lax.div(me, per)

    def v_of(t):
        return v_ref.at[:, pl.ds(pl.multiple_of(t * 128, 128), 128)]

    def got(place, sem):
        pltpu.make_async_copy(place, place, sem).wait()

    def send_all(source, target, sent, arrived):
        def send(i, _):
            to = lax.rem(me + i, width)
            pltpu.make_async_remote_copy(
                source(to),
                target.at[my_rows],
                sent.at[jnp.where(i <= EARLY, 0, 1)],
                arrived,
                device_id={"ctx": to},
                device_id_type=MESH,
            ).start()
            return 0

        lax.fori_loop(1, width, send, 0)
        pltpu.make_async_copy(source(me), target.at[my_rows], arrived).start()

    def send_clean(source, target, sent, which):
        def copy_to(to, sem):
            return pltpu.make_async_remote_copy(
                source(to),
                target.at[my_rows],
                sem,
                hold_got.at[which],
                device_id={"step": lax.rem(my_block + to, groups), "ctx": to},
                device_id_type=MESH,
            )

        def send(i, _):
            copy_to(lax.rem(me + i, width), sent.at[jnp.where(i <= EARLY, 0, 1)]).start()
            return 0

        lax.fori_loop(1, width, send, 0)

        @pl.when(own_holder)
        def _():
            pltpu.make_async_copy(source(me), target.at[my_rows], hold_got.at[which]).start()

        @pl.when(jnp.logical_not(own_holder))
        def _():
            copy_to(me, first_sent.at[which]).start()

    own_holder = lax.rem(my_block + me, groups) == g

    def send_q():
        send_all(lambda t: q_out.at[t], qh, q_sent, q_got.at[my_block])

    def send_k():
        send_all(lambda t: k_out.at[t], kh, k_sent, kv_got.at[0])

    def send_v():
        send_all(v_of, vh, v_sent, kv_got.at[1])

    def hand_on(target, which):
        part = target.at[pl.ds(pl.multiple_of(held * BLOCK, BLOCK), BLOCK)]
        got(part, hold_got.at[which])

        def send(i, _):
            pltpu.make_async_remote_copy(
                part,
                part,
                c_sent.at[which],
                c_got.at[which],
                device_id={"step": lax.rem(g + i, groups)},
                device_id_type=MESH,
            ).start()
            return 0

        lax.fori_loop(1, groups, send, 0)

    others = kc.at[pl.ds(0, (groups - 1) * BLOCK)]
    early = qh.at[pl.ds(0, EARLY * rows)]
    late = qh.at[pl.ds(0, (width - 1 - EARLY) * rows)]

    @pl.when(jnp.logical_not(clean))
    def _():
        send_q()
        got(early, q_sent.at[0])
        send_k()
        send_v()

    @pl.when(clean)
    def _():
        pl.semaphore_wait(all_in, groups - 1)
        send_clean(lambda t: k_out.at[t], kc, k_sent, 0)
        got(early, k_sent.at[0])
        send_clean(v_of, vc, v_sent, 1)
        hand_on(kc, 0)
        got(early, v_sent.at[0])
        send_q()
        hand_on(vc, 1)

    latent_copy = pltpu.make_async_remote_copy(
        latent_ref, moved_ref, l_sent, l_got, device_id={"step": after}, device_id_type=MESH
    )
    latent_copy.start()

    loads[3].wait()
    turns = times_ref[g].astype(jnp.float32) * freq[0:128, :]
    gate[...] = jnp.sum(
        jnp.cos(turns) * tw[0:128, :].astype(jnp.float32) + jnp.sin(turns) * tw[128:256, :].astype(jnp.float32),
        axis=0,
        keepdims=True,
    )
    loads[4].wait()
    loads[5].wait()

    far = (2 - prefix_ref[g]).astype(jnp.float32) * FAR
    ones = jnp.ones((CHUNK, 128), jnp.bfloat16)

    def attend(state, q, keys, values, start, stop, masked):
        for at in range(start, stop, CHUNK):
            s = lax.dot_general(
                q, keys[at : at + CHUNK, :], (((1,), (1,)), ((), ())), preferred_element_type=jnp.float32
            )
            top = jnp.max(s, axis=1, keepdims=True)
            if masked:
                top = top - far
            if state is not None:
                old, total_so_far = state
                top = jnp.maximum(old, top)
            p = jnp.exp2(s - (top + far if masked else top)).astype(jnp.bfloat16)
            mixed = jnp.dot(
                p, jnp.concatenate([values[at : at + CHUNK, :], ones], axis=1), preferred_element_type=jnp.float32
            )
            if state is not None:
                mixed = mixed + total_so_far * jnp.exp2(old - top)
            state = top, mixed
        return state

    def step(i, _):
        first = jnp.where(clean, lax.rem(i, 2) == 0, i < blocks)
        count = jnp.where(clean, lax.div(i, 2), lax.rem(i, blocks))
        block = lax.rem(my_block + 2 * blocks - 1 - count, blocks)
        here = pl.ds(pl.multiple_of(block * BLOCK, BLOCK), BLOCK)

        @pl.when(jnp.logical_and(jnp.logical_not(clean), i == PASS_KEYS))
        def _():
            hand_on(kc, 0)

        @pl.when(jnp.logical_and(jnp.logical_not(clean), i == PASS_VALUES))
        def _():
            hand_on(vc, 1)

        @pl.when(i == jnp.where(clean, 1, blocks))
        def _():
            pl.semaphore_wait(next_in, 1)
            got(others, c_got.at[0])
            got(others, c_got.at[1])

        @pl.when(jnp.logical_and(jnp.logical_not(clean), i == blocks))
        def _():
            got(kh, kv_got.at[0])
            got(vh, kv_got.at[1])

        @pl.when(first)
        def _():
            got(qh.at[here], q_got.at[block])
            q = qh[here, :]
            state = attend(None, q, ck, cv, total, 2 * total, False)
            top, mixed = attend(state, q, ck, cv, 0, total, True)
            acc[here, :] = mixed
            peak[here, :] = jnp.broadcast_to(top, (BLOCK, 128))

        @pl.when(jnp.logical_not(first))
        def _():
            q = qh[here, :]
            top, mixed = attend((peak[here, 0:1], acc[here, :]), q, kc, vc, 0, total, False)
            acc[here, :] = mixed
            peak[here, :] = jnp.broadcast_to(top, (BLOCK, 128))

            @pl.when(jnp.logical_not(clean))
            def _():
                _, mixed = attend((peak[here, 0:1], acc[here, :]), q, kh, vh, 0, total, False)
                acc[here, :] = mixed

            mixed = acc[here, :]
            mine[here, :] = (mixed[:, :128] / mixed[:, 128:] * gate[...]).astype(jnp.bfloat16)
            for s in range(per):
                owner = block * per + s
                pltpu.make_async_remote_copy(
                    mine.at[pl.ds(pl.multiple_of(owner * rows, rows), rows)],
                    gated_ref.at[:, pl.ds(pl.multiple_of(me * 128, 128), 128)],
                    o_sent,
                    o_got,
                    device_id={"step": after, "ctx": owner},
                    device_id_type=MESH,
                ).start()

        return 0

    lax.fori_loop(0, 2 * blocks, step, 0)

    @pl.when(clean)
    def _():
        got(early, q_sent.at[0])

    @pl.when(jnp.logical_not(clean))
    def _():
        got(early, k_sent.at[0])
        got(early, v_sent.at[0])

    for sent in (q_sent, k_sent, v_sent):
        got(late, sent.at[1])
    for which in range(2):
        got(others, c_sent.at[which])

        @pl.when(jnp.logical_and(clean, jnp.logical_not(own_holder)))
        def _():
            got(qh.at[pl.ds(0, rows)], first_sent.at[which])

    latent_copy.wait()
    got(mine, o_sent)
    got(gated_ref, o_got)


def body(latent, q, k, v, cache_keys, cache_values, time_weight, timestep, span_index, prefix_spans):
    rows, width = q.shape[1:]
    total = cache_keys.shape[0] // 2
    half = jnp.bfloat16
    smem = pl.BlockSpec(memory_space=pltpu.SMEM)
    hbm = pl.BlockSpec(memory_space=pl.ANY)
    dma = pltpu.SemaphoreType.DMA
    freqs = table()
    moved, gated = pl.pallas_call(
        kernel,
        out_shape=[jax.ShapeDtypeStruct((rows, width), half)] * 2,
        in_specs=[smem] * 3 + [hbm] * 8,
        out_specs=[hbm] * 2,
        scratch_shapes=[
            pltpu.VMEM(freqs.shape, jnp.float32),
            pltpu.VMEM((rows, width), half),
            pltpu.VMEM((rows, width), half),
            pltpu.VMEM((2 * total, 128), half),
            pltpu.VMEM((2 * total, 128), half),
            pltpu.VMEM((FREQS, 128), half),
            pltpu.VMEM((width // 128, rows, 128), half),
            pltpu.VMEM((width // 128, rows, 128), half),
            pltpu.VMEM((total, 128), half),
            pltpu.VMEM((total, 128), half),
            pltpu.VMEM((total, 128), half),
            pltpu.VMEM((total, 128), half),
            pltpu.VMEM((total, 128), half),
            pltpu.VMEM((total, 256), jnp.float32),
            pltpu.VMEM((total, 128), jnp.float32),
            pltpu.VMEM((1, 128), jnp.float32),
            pltpu.VMEM((total, 128), half),
            dma((6,)),
            dma((2,)),
            dma((2,)),
            dma((2,)),
            dma((total // BLOCK,)),
            dma((2,)),
            dma((2,)),
            dma((2,)),
            dma((2,)),
            dma((2,)),
            dma,
            dma,
            dma,
            dma,
            pltpu.SemaphoreType.REGULAR,
            pltpu.SemaphoreType.REGULAR,
        ],
        compiler_params=pltpu.CompilerParams(
            collective_id=0, has_side_effects=True, vmem_limit_bytes=56 * 1024 * 1024
        ),
    )(timestep, span_index, prefix_spans, jnp.asarray(freqs), latent[0], q[0], k[0], v[0], cache_keys, cache_values, time_weight)
    advanced = (moved.astype(jnp.float32) + gated.astype(jnp.float32)).astype(half)
    return advanced[None]


def solution(mesh):
    spans = P("step", "ctx", None)
    heads = P(None, "ctx")
    return jax.shard_map(
        body,
        mesh=mesh,
        in_specs=(spans,) * 4 + (heads,) * 3 + (P(),) * 3,
        out_specs=spans,
        check_vma=False,
    )
```

```python
import functools
import math

import jax
import jax.numpy as jnp
import numpy as np
from jax import lax
from jax.experimental import pallas as pl
from jax.experimental.pallas import tpu as pltpu
from jax.sharding import PartitionSpec as P

MESH = pl.DeviceIdType.MESH
HEAD_DIM = 128
FREQS = 256
FRAMES = 3
BLOCK = 256
CHUNK = 512
FAR = 1e30


EARLY = 24
PASS_KEYS = 2
PASS_VALUES = 8


def table():
    n = FREQS // 2
    gate = 10000.0 ** (-np.arange(n, dtype=np.float64) / n)
    half = HEAD_DIM // 2
    turn = 10000.0 ** (-np.arange(half, dtype=np.float64) / half)
    rows = np.concatenate([np.repeat(gate[:, None], 128, 1), np.repeat(np.tile(turn, 2)[None], 8, 0)])
    return rows.astype(np.float32)


def kernel(
    times_ref, spans_ref, prefix_ref, freq_ref, latent_ref, q_ref, k_ref, v_ref, ck_ref, cv_ref, tw_ref,
    moved_ref, gated_ref,
    freq, q_in, k_in, ck, cv, tw, q_out, k_out, qh, kh, vh, kc, vc, acc, peak, gate, mine,
    load_sem, q_sent, k_sent, v_sent, q_got, kv_got, hold_got, first_sent, c_sent, c_got, o_sent, o_got, l_sent, l_got, next_in, all_in,
):
    groups, width = lax.axis_size("step"), lax.axis_size("ctx")
    g, me = lax.axis_index("step"), lax.axis_index("ctx")
    rows = q_ref.shape[0]
    total = rows * width
    blocks = total // BLOCK
    per = BLOCK // rows
    last = groups - 1
    clean = g == last
    after, before = lax.rem(g + 1, groups), lax.rem(g + groups - 1, groups)
    held = lax.rem(g + groups * width - me, groups)

    loads = [
        pltpu.make_async_copy(a, b, load_sem.at[i])
        for i, (a, b) in enumerate(
            ((q_ref, q_in), (k_ref, k_in), (freq_ref, freq), (tw_ref, tw), (ck_ref, ck), (cv_ref, cv))
        )
    ]
    for load in loads:
        load.start()

    barrier = pltpu.get_barrier_semaphore()

    def greet(i, _):
        pl.semaphore_signal(barrier, inc=1, device_id={"ctx": lax.rem(me + i, width)}, device_id_type=MESH)
        return 0

    lax.fori_loop(1, width, greet, 0)

    def greet_step(i, _):
        pl.semaphore_signal(barrier, inc=1, device_id={"step": lax.rem(g + i, groups)}, device_id_type=MESH)
        return 0

    lax.fori_loop(1, groups, greet_step, 0)

    loads[2].wait()
    row = me * rows + lax.broadcasted_iota(jnp.int32, (rows, 128), 0)
    frames = spans_ref[g] * FRAMES + lax.div(row * FRAMES, total)
    angles = frames.astype(jnp.float32) * freq[128:129, :]
    cosine = jnp.cos(angles)
    lane = lax.broadcasted_iota(jnp.int32, (rows, 128), 1)
    sine = jnp.where(lane < HEAD_DIM // 2, -jnp.sin(angles), jnp.sin(angles))
    scale = math.log2(math.e) / math.sqrt(HEAD_DIM)
    loads[0].wait()
    loads[1].wait()

    def turn(h, _):
        cols = pl.ds(pl.multiple_of(h * 128, 128), 128)
        q = q_in[:, cols].astype(jnp.float32)
        k = k_in[:, cols].astype(jnp.float32)
        q_out[h] = ((q * cosine + pltpu.roll(q, 64, 1) * sine) * scale).astype(jnp.bfloat16)
        k_out[h] = (k * cosine + pltpu.roll(k, 64, 1) * sine).astype(jnp.bfloat16)
        return 0

    lax.fori_loop(0, width, turn, 0)
    pl.semaphore_wait(barrier, width + groups - 2)
    pl.semaphore_signal(next_in, inc=1, device_id={"step": before}, device_id_type=MESH)

    @pl.when(jnp.logical_not(clean))
    def _():
        pl.semaphore_signal(all_in, inc=1, device_id={"step": last}, device_id_type=MESH)

    my_rows = pl.ds(pl.multiple_of(me * rows, rows), rows)
    my_block = lax.div(me, per)

    def v_of(t):
        return v_ref.at[:, pl.ds(pl.multiple_of(t * 128, 128), 128)]

    def got(place, sem):
        pltpu.make_async_copy(place, place, sem).wait()

    def send_all(source, target, sent, arrived):
        def send(i, _):
            to = lax.rem(me + i, width)
            pltpu.make_async_remote_copy(
                source(to),
                target.at[my_rows],
                sent.at[jnp.where(i <= EARLY, 0, 1)],
                arrived,
                device_id={"ctx": to},
                device_id_type=MESH,
            ).start()
            return 0

        lax.fori_loop(1, width, send, 0)
        pltpu.make_async_copy(source(me), target.at[my_rows], arrived).start()

    def send_clean(source, target, sent, which):
        def copy_to(to, sem):
            return pltpu.make_async_remote_copy(
                source(to),
                target.at[my_rows],
                sem,
                hold_got.at[which],
                device_id={"step": lax.rem(my_block + to, groups), "ctx": to},
                device_id_type=MESH,
            )

        def send(i, _):
            copy_to(lax.rem(me + i, width), sent.at[jnp.where(i <= EARLY, 0, 1)]).start()
            return 0

        lax.fori_loop(1, width, send, 0)

        @pl.when(own_holder)
        def _():
            pltpu.make_async_copy(source(me), target.at[my_rows], hold_got.at[which]).start()

        @pl.when(jnp.logical_not(own_holder))
        def _():
            copy_to(me, first_sent.at[which]).start()

    own_holder = lax.rem(my_block + me, groups) == g

    def send_q():
        send_all(lambda t: q_out.at[t], qh, q_sent, q_got.at[my_block])

    def send_k():
        send_all(lambda t: k_out.at[t], kh, k_sent, kv_got.at[0])

    def send_v():
        send_all(v_of, vh, v_sent, kv_got.at[1])

    def hand_on(target, which):
        part = target.at[pl.ds(pl.multiple_of(held * BLOCK, BLOCK), BLOCK)]
        got(part, hold_got.at[which])

        def send(i, _):
            pltpu.make_async_remote_copy(
                part,
                part,
                c_sent.at[which],
                c_got.at[which],
                device_id={"step": lax.rem(g + i, groups)},
                device_id_type=MESH,
            ).start()
            return 0

        lax.fori_loop(1, groups, send, 0)

    others = kc.at[pl.ds(0, (groups - 1) * BLOCK)]
    early = qh.at[pl.ds(0, EARLY * rows)]
    late = qh.at[pl.ds(0, (width - 1 - EARLY) * rows)]

    @pl.when(jnp.logical_not(clean))
    def _():
        send_q()
        send_k()
        send_v()

    @pl.when(clean)
    def _():
        pl.semaphore_wait(all_in, groups - 1)
        send_clean(lambda t: k_out.at[t], kc, k_sent, 0)
        send_clean(v_of, vc, v_sent, 1)
        send_q()
        got(early, k_sent.at[0])
        got(early, v_sent.at[0])
        hand_on(kc, 0)
        hand_on(vc, 1)

    latent_copy = pltpu.make_async_remote_copy(
        latent_ref, moved_ref, l_sent, l_got, device_id={"step": after}, device_id_type=MESH
    )
    latent_copy.start()

    loads[3].wait()
    turns = times_ref[g].astype(jnp.float32) * freq[0:128, :]
    gate[...] = jnp.sum(
        jnp.cos(turns) * tw[0:128, :].astype(jnp.float32) + jnp.sin(turns) * tw[128:256, :].astype(jnp.float32),
        axis=0,
        keepdims=True,
    )
    loads[4].wait()
    loads[5].wait()

    far = (2 - prefix_ref[g]).astype(jnp.float32) * FAR
    ones = jnp.ones((CHUNK, 128), jnp.bfloat16)

    def attend(state, q, keys, values, start, stop, masked):
        for at in range(start, stop, CHUNK):
            s = lax.dot_general(
                q, keys[at : at + CHUNK, :], (((1,), (1,)), ((), ())), preferred_element_type=jnp.float32
            )
            top = jnp.max(s, axis=1, keepdims=True)
            if masked:
                top = top - far
            if state is not None:
                old, total_so_far = state
                top = jnp.maximum(old, top)
            p = jnp.exp2(s - (top + far if masked else top)).astype(jnp.bfloat16)
            mixed = jnp.dot(
                p, jnp.concatenate([values[at : at + CHUNK, :], ones], axis=1), preferred_element_type=jnp.float32
            )
            if state is not None:
                mixed = mixed + total_so_far * jnp.exp2(old - top)
            state = top, mixed
        return state

    def step(i, _):
        first = i < blocks
        count = lax.rem(i, blocks)
        block = lax.rem(my_block + 2 * blocks - 1 - count, blocks)
        here = pl.ds(pl.multiple_of(block * BLOCK, BLOCK), BLOCK)

        @pl.when(jnp.logical_and(jnp.logical_not(clean), i == PASS_KEYS))
        def _():
            hand_on(kc, 0)

        @pl.when(jnp.logical_and(jnp.logical_not(clean), i == PASS_VALUES))
        def _():
            hand_on(vc, 1)

        @pl.when(i == blocks)
        def _():
            pl.semaphore_wait(next_in, 1)
            got(others, c_got.at[0])
            got(others, c_got.at[1])

        @pl.when(jnp.logical_and(jnp.logical_not(clean), i == blocks))
        def _():
            got(kh, kv_got.at[0])
            got(vh, kv_got.at[1])

        @pl.when(first)
        def _():
            got(qh.at[here], q_got.at[block])
            q = qh[here, :]
            state = attend(None, q, ck, cv, total, 2 * total, False)
            top, mixed = attend(state, q, ck, cv, 0, total, True)
            acc[here, :] = mixed
            peak[here, :] = jnp.broadcast_to(top, (BLOCK, 128))

        @pl.when(jnp.logical_not(first))
        def _():
            q = qh[here, :]
            top, mixed = attend((peak[here, 0:1], acc[here, :]), q, kc, vc, 0, total, False)
            acc[here, :] = mixed
            peak[here, :] = jnp.broadcast_to(top, (BLOCK, 128))

            @pl.when(jnp.logical_not(clean))
            def _():
                _, mixed = attend((peak[here, 0:1], acc[here, :]), q, kh, vh, 0, total, False)
                acc[here, :] = mixed

            mixed = acc[here, :]
            mine[here, :] = (mixed[:, :128] / mixed[:, 128:] * gate[...]).astype(jnp.bfloat16)
            for s in range(per):
                owner = block * per + s
                pltpu.make_async_remote_copy(
                    mine.at[pl.ds(pl.multiple_of(owner * rows, rows), rows)],
                    gated_ref.at[:, pl.ds(pl.multiple_of(me * 128, 128), 128)],
                    o_sent,
                    o_got,
                    device_id={"step": after, "ctx": owner},
                    device_id_type=MESH,
                ).start()

        return 0

    lax.fori_loop(0, 2 * blocks, step, 0)

    @pl.when(clean)
    def _():
        got(early, q_sent.at[0])

    @pl.when(jnp.logical_not(clean))
    def _():
        got(early, k_sent.at[0])
        got(early, v_sent.at[0])

    @pl.when(jnp.logical_not(clean))
    def _():
        got(early, q_sent.at[0])

    for sent in (q_sent, k_sent, v_sent):
        got(late, sent.at[1])
    for which in range(2):
        got(others, c_sent.at[which])

        @pl.when(jnp.logical_and(clean, jnp.logical_not(own_holder)))
        def _():
            got(qh.at[pl.ds(0, rows)], first_sent.at[which])

    latent_copy.wait()
    got(mine, o_sent)
    got(gated_ref, o_got)


def body(latent, q, k, v, cache_keys, cache_values, time_weight, timestep, span_index, prefix_spans):
    rows, width = q.shape[1:]
    total = cache_keys.shape[0] // 2
    half = jnp.bfloat16
    smem = pl.BlockSpec(memory_space=pltpu.SMEM)
    hbm = pl.BlockSpec(memory_space=pl.ANY)
    dma = pltpu.SemaphoreType.DMA
    freqs = table()
    moved, gated = pl.pallas_call(
        kernel,
        out_shape=[jax.ShapeDtypeStruct((rows, width), half)] * 2,
        in_specs=[smem] * 3 + [hbm] * 8,
        out_specs=[hbm] * 2,
        scratch_shapes=[
            pltpu.VMEM(freqs.shape, jnp.float32),
            pltpu.VMEM((rows, width), half),
            pltpu.VMEM((rows, width), half),
            pltpu.VMEM((2 * total, 128), half),
            pltpu.VMEM((2 * total, 128), half),
            pltpu.VMEM((FREQS, 128), half),
            pltpu.VMEM((width // 128, rows, 128), half),
            pltpu.VMEM((width // 128, rows, 128), half),
            pltpu.VMEM((total, 128), half),
            pltpu.VMEM((total, 128), half),
            pltpu.VMEM((total, 128), half),
            pltpu.VMEM((total, 128), half),
            pltpu.VMEM((total, 128), half),
            pltpu.VMEM((total, 256), jnp.float32),
            pltpu.VMEM((total, 128), jnp.float32),
            pltpu.VMEM((1, 128), jnp.float32),
            pltpu.VMEM((total, 128), half),
            dma((6,)),
            dma((2,)),
            dma((2,)),
            dma((2,)),
            dma((total // BLOCK,)),
            dma((2,)),
            dma((2,)),
            dma((2,)),
            dma((2,)),
            dma((2,)),
            dma,
            dma,
            dma,
            dma,
            pltpu.SemaphoreType.REGULAR,
            pltpu.SemaphoreType.REGULAR,
        ],
        compiler_params=pltpu.CompilerParams(
            collective_id=0, has_side_effects=True, vmem_limit_bytes=56 * 1024 * 1024
        ),
    )(timestep, span_index, prefix_spans, jnp.asarray(freqs), latent[0], q[0], k[0], v[0], cache_keys, cache_values, time_weight)
    advanced = (moved.astype(jnp.float32) + gated.astype(jnp.float32)).astype(half)
    return advanced[None]


def solution(mesh):
    spans = P("step", "ctx", None)
    heads = P(None, "ctx")
    return jax.shard_map(
        body,
        mesh=mesh,
        in_specs=(spans,) * 4 + (heads,) * 3 + (P(),) * 3,
        out_specs=spans,
        check_vma=False,
    )
```

```python
import functools
import math

import jax
import jax.numpy as jnp
import numpy as np
from jax import lax
from jax.experimental import pallas as pl
from jax.experimental.pallas import tpu as pltpu
from jax.sharding import PartitionSpec as P

MESH = pl.DeviceIdType.MESH
HEAD_DIM = 128
FREQS = 256
FRAMES = 3
BLOCK = 256
CHUNK = 512
FAR = 1e30


EARLY = 24
PASS_KEYS = 2
PASS_VALUES = 8


def table():
    n = FREQS // 2
    gate = 10000.0 ** (-np.arange(n, dtype=np.float64) / n)
    half = HEAD_DIM // 2
    turn = 10000.0 ** (-np.arange(half, dtype=np.float64) / half)
    rows = np.concatenate([np.repeat(gate[:, None], 128, 1), np.repeat(np.tile(turn, 2)[None], 8, 0)])
    return rows.astype(np.float32)


def kernel(
    times_ref, spans_ref, prefix_ref, freq_ref, latent_ref, q_ref, k_ref, v_ref, ck_ref, cv_ref, tw_ref,
    moved_ref, gated_ref,
    freq, q_in, k_in, ck, cv, tw, q_out, k_out, qh, kh, vh, kc, vc, acc, peak, gate, mine,
    load_sem, q_sent, k_sent, v_sent, q_got, kv_got, hold_got, first_sent, c_sent, c_got, o_sent, o_got, l_sent, l_got, next_in, all_in,
):
    groups, width = lax.axis_size("step"), lax.axis_size("ctx")
    g, me = lax.axis_index("step"), lax.axis_index("ctx")
    rows = q_ref.shape[0]
    total = rows * width
    blocks = total // BLOCK
    per = BLOCK // rows
    last = groups - 1
    clean = g == last
    after, before = lax.rem(g + 1, groups), lax.rem(g + groups - 1, groups)
    held = lax.rem(g + groups * width - me, groups)

    loads = [
        pltpu.make_async_copy(a, b, load_sem.at[i])
        for i, (a, b) in enumerate(
            ((q_ref, q_in), (k_ref, k_in), (freq_ref, freq), (tw_ref, tw), (ck_ref, ck), (cv_ref, cv))
        )
    ]
    for load in loads:
        load.start()

    barrier = pltpu.get_barrier_semaphore()

    def greet(i, _):
        pl.semaphore_signal(barrier, inc=1, device_id={"ctx": lax.rem(me + i, width)}, device_id_type=MESH)
        return 0

    lax.fori_loop(1, width, greet, 0)

    def greet_step(i, _):
        pl.semaphore_signal(barrier, inc=1, device_id={"step": lax.rem(g + i, groups)}, device_id_type=MESH)
        return 0

    lax.fori_loop(1, groups, greet_step, 0)

    loads[2].wait()
    row = me * rows + lax.broadcasted_iota(jnp.int32, (rows, 128), 0)
    frames = spans_ref[g] * FRAMES + lax.div(row * FRAMES, total)
    angles = frames.astype(jnp.float32) * freq[128:129, :]
    cosine = jnp.cos(angles)
    lane = lax.broadcasted_iota(jnp.int32, (rows, 128), 1)
    sine = jnp.where(lane < HEAD_DIM // 2, -jnp.sin(angles), jnp.sin(angles))
    scale = math.log2(math.e) / math.sqrt(HEAD_DIM)
    loads[0].wait()
    loads[1].wait()

    def turn(h, _):
        cols = pl.ds(pl.multiple_of(h * 128, 128), 128)
        q = q_in[:, cols].astype(jnp.float32)
        k = k_in[:, cols].astype(jnp.float32)
        q_out[h] = ((q * cosine + pltpu.roll(q, 64, 1) * sine) * scale).astype(jnp.bfloat16)
        k_out[h] = (k * cosine + pltpu.roll(k, 64, 1) * sine).astype(jnp.bfloat16)
        return 0

    lax.fori_loop(0, width, turn, 0)
    pl.semaphore_wait(barrier, width + groups - 2)
    pl.semaphore_signal(next_in, inc=1, device_id={"step": before}, device_id_type=MESH)

    @pl.when(jnp.logical_not(clean))
    def _():
        pl.semaphore_signal(all_in, inc=1, device_id={"step": last}, device_id_type=MESH)

    my_rows = pl.ds(pl.multiple_of(me * rows, rows), rows)
    my_block = lax.div(me, per)

    def v_of(t):
        return v_ref.at[:, pl.ds(pl.multiple_of(t * 128, 128), 128)]

    def got(place, sem):
        pltpu.make_async_copy(place, place, sem).wait()

    def send_all(source, target, sent, arrived):
        def send(i, _):
            to = lax.rem(me + i, width)
            pltpu.make_async_remote_copy(
                source(to),
                target.at[my_rows],
                sent.at[jnp.where(i <= EARLY, 0, 1)],
                arrived,
                device_id={"ctx": to},
                device_id_type=MESH,
            ).start()
            return 0

        lax.fori_loop(1, width, send, 0)
        pltpu.make_async_copy(source(me), target.at[my_rows], arrived).start()

    def send_clean(source, target, sent, which):
        def copy_to(to, sem):
            return pltpu.make_async_remote_copy(
                source(to),
                target.at[my_rows],
                sem,
                hold_got.at[which],
                device_id={"step": lax.rem(my_block + to, groups), "ctx": to},
                device_id_type=MESH,
            )

        def send(i, _):
            copy_to(lax.rem(me + i, width), sent.at[jnp.where(i <= EARLY, 0, 1)]).start()
            return 0

        lax.fori_loop(1, width, send, 0)

        @pl.when(own_holder)
        def _():
            pltpu.make_async_copy(source(me), target.at[my_rows], hold_got.at[which]).start()

        @pl.when(jnp.logical_not(own_holder))
        def _():
            copy_to(me, first_sent.at[which]).start()

    own_holder = lax.rem(my_block + me, groups) == g

    def send_q():
        send_all(lambda t: q_out.at[t], qh, q_sent, q_got.at[my_block])

    def send_k():
        send_all(lambda t: k_out.at[t], kh, k_sent, kv_got.at[0])

    def send_v():
        send_all(v_of, vh, v_sent, kv_got.at[1])

    def hand_on(target, which):
        part = target.at[pl.ds(pl.multiple_of(held * BLOCK, BLOCK), BLOCK)]
        got(part, hold_got.at[which])

        def send(i, _):
            pltpu.make_async_remote_copy(
                part,
                part,
                c_sent.at[which],
                c_got.at[which],
                device_id={"step": lax.rem(g + i, groups)},
                device_id_type=MESH,
            ).start()
            return 0

        lax.fori_loop(1, groups, send, 0)

    others = kc.at[pl.ds(0, (groups - 1) * BLOCK)]
    early = qh.at[pl.ds(0, EARLY * rows)]
    late = qh.at[pl.ds(0, (width - 1 - EARLY) * rows)]

    @pl.when(jnp.logical_not(clean))
    def _():
        send_q()
        send_k()
        send_v()

    @pl.when(clean)
    def _():
        pl.semaphore_wait(all_in, groups - 1)
        send_clean(lambda t: k_out.at[t], kc, k_sent, 0)
        send_clean(v_of, vc, v_sent, 1)
        send_q()
        got(early, k_sent.at[0])
        got(early, v_sent.at[0])
        hand_on(kc, 0)
        hand_on(vc, 1)

    latent_copy = pltpu.make_async_remote_copy(
        latent_ref, moved_ref, l_sent, l_got, device_id={"step": after}, device_id_type=MESH
    )
    latent_copy.start()

    loads[3].wait()
    turns = times_ref[g].astype(jnp.float32) * freq[0:128, :]
    gate[...] = jnp.sum(
        jnp.cos(turns) * tw[0:128, :].astype(jnp.float32) + jnp.sin(turns) * tw[128:256, :].astype(jnp.float32),
        axis=0,
        keepdims=True,
    )
    loads[4].wait()
    loads[5].wait()

    far = (2 - prefix_ref[g]).astype(jnp.float32) * FAR
    ones = jnp.ones((CHUNK, 128), jnp.bfloat16)

    def attend(state, q, keys, values, start, stop, masked):
        for at in range(start, stop, CHUNK):
            s = lax.dot_general(
                q, keys[at : at + CHUNK, :], (((1,), (1,)), ((), ())), preferred_element_type=jnp.float32
            )
            top = jnp.max(s, axis=1, keepdims=True)
            if masked:
                top = top - far
            if state is not None:
                old, total_so_far = state
                top = jnp.maximum(old, top)
            p = jnp.exp2(s - (top + far if masked else top)).astype(jnp.bfloat16)
            mixed = jnp.dot(
                p, jnp.concatenate([values[at : at + CHUNK, :], ones], axis=1), preferred_element_type=jnp.float32
            )
            if state is not None:
                mixed = mixed + total_so_far * jnp.exp2(old - top)
            state = top, mixed
        return state

    def step(i, _):
        first, final = i < blocks, i >= 2 * blocks
        count = lax.rem(i, blocks)
        block = lax.rem(my_block + 2 * blocks - 1 - count, blocks)
        here = pl.ds(pl.multiple_of(block * BLOCK, BLOCK), BLOCK)

        @pl.when(jnp.logical_and(jnp.logical_not(clean), i == PASS_KEYS))
        def _():
            hand_on(kc, 0)

        @pl.when(jnp.logical_and(jnp.logical_not(clean), i == PASS_VALUES))
        def _():
            hand_on(vc, 1)

        @pl.when(jnp.logical_and(jnp.logical_not(clean), i == blocks))
        def _():
            got(kh, kv_got.at[0])
            got(vh, kv_got.at[1])

        @pl.when(i == 2 * blocks)
        def _():
            pl.semaphore_wait(next_in, 1)
            got(others, c_got.at[0])
            got(others, c_got.at[1])

        @pl.when(first)
        def _():
            got(qh.at[here], q_got.at[block])
            q = qh[here, :]
            state = attend(None, q, ck, cv, total, 2 * total, False)
            top, mixed = attend(state, q, ck, cv, 0, total, True)
            acc[here, :] = mixed
            peak[here, :] = jnp.broadcast_to(top, (BLOCK, 128))

        @pl.when(jnp.logical_not(jnp.logical_or(jnp.logical_or(first, final), clean)))
        def _():
            q = qh[here, :]
            top, mixed = attend((peak[here, 0:1], acc[here, :]), q, kh, vh, 0, total, False)
            acc[here, :] = mixed
            peak[here, :] = jnp.broadcast_to(top, (BLOCK, 128))

        @pl.when(final)
        def _():
            q = qh[here, :]
            _, mixed = attend((peak[here, 0:1], acc[here, :]), q, kc, vc, 0, total, False)
            mine[here, :] = (mixed[:, :128] / mixed[:, 128:] * gate[...]).astype(jnp.bfloat16)
            for s in range(per):
                owner = block * per + s
                pltpu.make_async_remote_copy(
                    mine.at[pl.ds(pl.multiple_of(owner * rows, rows), rows)],
                    gated_ref.at[:, pl.ds(pl.multiple_of(me * 128, 128), 128)],
                    o_sent,
                    o_got,
                    device_id={"step": after, "ctx": owner},
                    device_id_type=MESH,
                ).start()

        return 0

    lax.fori_loop(0, 3 * blocks, step, 0)

    @pl.when(clean)
    def _():
        got(early, q_sent.at[0])

    @pl.when(jnp.logical_not(clean))
    def _():
        got(early, k_sent.at[0])
        got(early, v_sent.at[0])

    @pl.when(jnp.logical_not(clean))
    def _():
        got(early, q_sent.at[0])

    for sent in (q_sent, k_sent, v_sent):
        got(late, sent.at[1])
    for which in range(2):
        got(others, c_sent.at[which])

        @pl.when(jnp.logical_and(clean, jnp.logical_not(own_holder)))
        def _():
            got(qh.at[pl.ds(0, rows)], first_sent.at[which])

    latent_copy.wait()
    got(mine, o_sent)
    got(gated_ref, o_got)


def body(latent, q, k, v, cache_keys, cache_values, time_weight, timestep, span_index, prefix_spans):
    rows, width = q.shape[1:]
    total = cache_keys.shape[0] // 2
    half = jnp.bfloat16
    smem = pl.BlockSpec(memory_space=pltpu.SMEM)
    hbm = pl.BlockSpec(memory_space=pl.ANY)
    dma = pltpu.SemaphoreType.DMA
    freqs = table()
    moved, gated = pl.pallas_call(
        kernel,
        out_shape=[jax.ShapeDtypeStruct((rows, width), half)] * 2,
        in_specs=[smem] * 3 + [hbm] * 8,
        out_specs=[hbm] * 2,
        scratch_shapes=[
            pltpu.VMEM(freqs.shape, jnp.float32),
            pltpu.VMEM((rows, width), half),
            pltpu.VMEM((rows, width), half),
            pltpu.VMEM((2 * total, 128), half),
            pltpu.VMEM((2 * total, 128), half),
            pltpu.VMEM((FREQS, 128), half),
            pltpu.VMEM((width // 128, rows, 128), half),
            pltpu.VMEM((width // 128, rows, 128), half),
            pltpu.VMEM((total, 128), half),
            pltpu.VMEM((total, 128), half),
            pltpu.VMEM((total, 128), half),
            pltpu.VMEM((total, 128), half),
            pltpu.VMEM((total, 128), half),
            pltpu.VMEM((total, 256), jnp.float32),
            pltpu.VMEM((total, 128), jnp.float32),
            pltpu.VMEM((1, 128), jnp.float32),
            pltpu.VMEM((total, 128), half),
            dma((6,)),
            dma((2,)),
            dma((2,)),
            dma((2,)),
            dma((total // BLOCK,)),
            dma((2,)),
            dma((2,)),
            dma((2,)),
            dma((2,)),
            dma((2,)),
            dma,
            dma,
            dma,
            dma,
            pltpu.SemaphoreType.REGULAR,
            pltpu.SemaphoreType.REGULAR,
        ],
        compiler_params=pltpu.CompilerParams(
            collective_id=0, has_side_effects=True, vmem_limit_bytes=56 * 1024 * 1024
        ),
    )(timestep, span_index, prefix_spans, jnp.asarray(freqs), latent[0], q[0], k[0], v[0], cache_keys, cache_values, time_weight)
    advanced = (moved.astype(jnp.float32) + gated.astype(jnp.float32)).astype(half)
    return advanced[None]


def solution(mesh):
    spans = P("step", "ctx", None)
    heads = P(None, "ctx")
    return jax.shard_map(
        body,
        mesh=mesh,
        in_specs=(spans,) * 4 + (heads,) * 3 + (P(),) * 3,
        out_specs=spans,
        check_vma=False,
    )
```

```python
import functools
import math

import jax
import jax.numpy as jnp
import numpy as np
from jax import lax
from jax.experimental import pallas as pl
from jax.experimental.pallas import tpu as pltpu
from jax.sharding import PartitionSpec as P

MESH = pl.DeviceIdType.MESH
HEAD_DIM = 128
FREQS = 256
FRAMES = 3
BLOCK = 256
CHUNK = 512
FAR = 1e30


EARLY = 24
PASS_KEYS = 2
PASS_VALUES = 8


def table():
    n = FREQS // 2
    gate = 10000.0 ** (-np.arange(n, dtype=np.float64) / n)
    half = HEAD_DIM // 2
    turn = 10000.0 ** (-np.arange(half, dtype=np.float64) / half)
    rows = np.concatenate([np.repeat(gate[:, None], 128, 1), np.repeat(np.tile(turn, 2)[None], 8, 0)])
    return rows.astype(np.float32)


def kernel(
    times_ref, spans_ref, prefix_ref, freq_ref, latent_ref, q_ref, k_ref, v_ref, ck_ref, cv_ref, tw_ref,
    moved_ref, gated_ref,
    freq, q_in, k_in, ck, cv, tw, q_out, k_out, qh, kh, vh, kc, vc, acc, peak, gate, mine,
    load_sem, q_sent, k_sent, v_sent, q_got, kv_got, hold_got, first_sent, c_sent, c_got, o_sent, o_got, l_sent, l_got, next_in, all_in,
):
    groups, width = lax.axis_size("step"), lax.axis_size("ctx")
    g, me = lax.axis_index("step"), lax.axis_index("ctx")
    rows = q_ref.shape[0]
    total = rows * width
    blocks = total // BLOCK
    per = BLOCK // rows
    last = groups - 1
    clean = g == last
    after, before = lax.rem(g + 1, groups), lax.rem(g + groups - 1, groups)
    held = lax.rem(g + groups * width - me, groups)

    loads = [
        pltpu.make_async_copy(a, b, load_sem.at[i])
        for i, (a, b) in enumerate(
            ((q_ref, q_in), (k_ref, k_in), (freq_ref, freq), (tw_ref, tw), (ck_ref, ck), (cv_ref, cv))
        )
    ]
    for load in loads:
        load.start()

    barrier = pltpu.get_barrier_semaphore()

    def greet(i, _):
        pl.semaphore_signal(barrier, inc=1, device_id={"ctx": lax.rem(me + i, width)}, device_id_type=MESH)
        return 0

    lax.fori_loop(1, width, greet, 0)

    def greet_step(i, _):
        pl.semaphore_signal(barrier, inc=1, device_id={"step": lax.rem(g + i, groups)}, device_id_type=MESH)
        return 0

    lax.fori_loop(1, groups, greet_step, 0)

    loads[2].wait()
    row = me * rows + lax.broadcasted_iota(jnp.int32, (rows, 128), 0)
    frames = spans_ref[g] * FRAMES + lax.div(row * FRAMES, total)
    angles = frames.astype(jnp.float32) * freq[128:129, :]
    cosine = jnp.cos(angles)
    lane = lax.broadcasted_iota(jnp.int32, (rows, 128), 1)
    sine = jnp.where(lane < HEAD_DIM // 2, -jnp.sin(angles), jnp.sin(angles))
    scale = math.log2(math.e) / math.sqrt(HEAD_DIM)
    loads[0].wait()
    loads[1].wait()

    def turn(h, _):
        cols = pl.ds(pl.multiple_of(h * 128, 128), 128)
        q = q_in[:, cols].astype(jnp.float32)
        k = k_in[:, cols].astype(jnp.float32)
        q_out[h] = ((q * cosine + pltpu.roll(q, 64, 1) * sine) * scale).astype(jnp.bfloat16)
        k_out[h] = (k * cosine + pltpu.roll(k, 64, 1) * sine).astype(jnp.bfloat16)
        return 0

    lax.fori_loop(0, width, turn, 0)
    pl.semaphore_wait(barrier, width + groups - 2)
    pl.semaphore_signal(next_in, inc=1, device_id={"step": before}, device_id_type=MESH)

    @pl.when(jnp.logical_not(clean))
    def _():
        pl.semaphore_signal(all_in, inc=1, device_id={"step": last}, device_id_type=MESH)

    my_rows = pl.ds(pl.multiple_of(me * rows, rows), rows)
    my_block = lax.div(me, per)

    def v_of(t):
        return v_ref.at[:, pl.ds(pl.multiple_of(t * 128, 128), 128)]

    def got(place, sem):
        pltpu.make_async_copy(place, place, sem).wait()

    def send_all(source, target, sent, arrived):
        def send(i, _):
            to = lax.rem(me + i, width)
            pltpu.make_async_remote_copy(
                source(to),
                target.at[my_rows],
                sent.at[jnp.where(i <= EARLY, 0, 1)],
                arrived,
                device_id={"ctx": to},
                device_id_type=MESH,
            ).start()
            return 0

        lax.fori_loop(1, width, send, 0)
        pltpu.make_async_copy(source(me), target.at[my_rows], arrived).start()

    def send_clean(source, target, sent, which):
        def copy_to(to, sem):
            return pltpu.make_async_remote_copy(
                source(to),
                target.at[my_rows],
                sem,
                hold_got.at[which],
                device_id={"step": lax.rem(my_block + to, groups), "ctx": to},
                device_id_type=MESH,
            )

        def send(i, _):
            copy_to(lax.rem(me + i, width), sent.at[jnp.where(i <= EARLY, 0, 1)]).start()
            return 0

        lax.fori_loop(1, width, send, 0)

        @pl.when(own_holder)
        def _():
            pltpu.make_async_copy(source(me), target.at[my_rows], hold_got.at[which]).start()

        @pl.when(jnp.logical_not(own_holder))
        def _():
            copy_to(me, first_sent.at[which]).start()

    own_holder = lax.rem(my_block + me, groups) == g

    def send_q():
        send_all(lambda t: q_out.at[t], qh, q_sent, q_got.at[my_block])

    def send_k():
        send_all(lambda t: k_out.at[t], kh, k_sent, kv_got.at[0])

    def send_v():
        send_all(v_of, vh, v_sent, kv_got.at[1])

    def hand_on(target, which):
        part = target.at[pl.ds(pl.multiple_of(held * BLOCK, BLOCK), BLOCK)]
        got(part, hold_got.at[which])

        def send(i, _):
            pltpu.make_async_remote_copy(
                part,
                part,
                c_sent.at[which],
                c_got.at[which],
                device_id={"step": lax.rem(g + i, groups)},
                device_id_type=MESH,
            ).start()
            return 0

        lax.fori_loop(1, groups, send, 0)

    others = kc.at[pl.ds(0, (groups - 1) * BLOCK)]
    early = qh.at[pl.ds(0, EARLY * rows)]
    late = qh.at[pl.ds(0, (width - 1 - EARLY) * rows)]

    latent_copy = pltpu.make_async_remote_copy(
        latent_ref, moved_ref, l_sent, l_got, device_id={"step": after}, device_id_type=MESH
    )
    latent_copy.start()

    @pl.when(jnp.logical_not(clean))
    def _():
        send_q()
        send_k()
        send_v()

    @pl.when(clean)
    def _():
        pl.semaphore_wait(all_in, groups - 1)
        send_clean(lambda t: k_out.at[t], kc, k_sent, 0)
        send_clean(v_of, vc, v_sent, 1)
        send_q()
        got(early, k_sent.at[0])
        got(early, v_sent.at[0])
        hand_on(kc, 0)
        hand_on(vc, 1)

    loads[3].wait()
    turns = times_ref[g].astype(jnp.float32) * freq[0:128, :]
    gate[...] = jnp.sum(
        jnp.cos(turns) * tw[0:128, :].astype(jnp.float32) + jnp.sin(turns) * tw[128:256, :].astype(jnp.float32),
        axis=0,
        keepdims=True,
    )
    loads[4].wait()
    loads[5].wait()

    far = (2 - prefix_ref[g]).astype(jnp.float32) * FAR
    ones = jnp.ones((CHUNK, 128), jnp.bfloat16)

    def attend(state, q, keys, values, start, stop, masked):
        for at in range(start, stop, CHUNK):
            s = lax.dot_general(
                q, keys[at : at + CHUNK, :], (((1,), (1,)), ((), ())), preferred_element_type=jnp.float32
            )
            top = jnp.max(s, axis=1, keepdims=True)
            if masked:
                top = top - far
            if state is not None:
                old, total_so_far = state
                top = jnp.maximum(old, top)
            p = jnp.exp2(s - (top + far if masked else top)).astype(jnp.bfloat16)
            mixed = jnp.dot(
                p, jnp.concatenate([values[at : at + CHUNK, :], ones], axis=1), preferred_element_type=jnp.float32
            )
            if state is not None:
                mixed = mixed + total_so_far * jnp.exp2(old - top)
            state = top, mixed
        return state

    def step(i, _):
        first, final = i < blocks, i >= 2 * blocks
        count = lax.rem(i, blocks)
        block = lax.rem(my_block + 2 * blocks - 1 - count, blocks)
        here = pl.ds(pl.multiple_of(block * BLOCK, BLOCK), BLOCK)

        @pl.when(jnp.logical_and(jnp.logical_not(clean), i == PASS_KEYS))
        def _():
            hand_on(kc, 0)

        @pl.when(jnp.logical_and(jnp.logical_not(clean), i == PASS_VALUES))
        def _():
            hand_on(vc, 1)

        @pl.when(jnp.logical_and(jnp.logical_not(clean), i == blocks))
        def _():
            got(kh, kv_got.at[0])
            got(vh, kv_got.at[1])

        @pl.when(i == 2 * blocks)
        def _():
            pl.semaphore_wait(next_in, 1)
            got(others, c_got.at[0])
            got(others, c_got.at[1])

        @pl.when(first)
        def _():
            got(qh.at[here], q_got.at[block])
            q = qh[here, :]
            state = attend(None, q, ck, cv, total, 2 * total, False)
            top, mixed = attend(state, q, ck, cv, 0, total, True)
            acc[here, :] = mixed
            peak[here, :] = jnp.broadcast_to(top, (BLOCK, 128))

        @pl.when(jnp.logical_not(jnp.logical_or(jnp.logical_or(first, final), clean)))
        def _():
            q = qh[here, :]
            top, mixed = attend((peak[here, 0:1], acc[here, :]), q, kh, vh, 0, total, False)
            acc[here, :] = mixed
            peak[here, :] = jnp.broadcast_to(top, (BLOCK, 128))

        @pl.when(final)
        def _():
            q = qh[here, :]
            _, mixed = attend((peak[here, 0:1], acc[here, :]), q, kc, vc, 0, total, False)
            mine[here, :] = (mixed[:, :128] / mixed[:, 128:] * gate[...]).astype(jnp.bfloat16)
            for s in range(per):
                owner = block * per + s
                pltpu.make_async_remote_copy(
                    mine.at[pl.ds(pl.multiple_of(owner * rows, rows), rows)],
                    gated_ref.at[:, pl.ds(pl.multiple_of(me * 128, 128), 128)],
                    o_sent,
                    o_got,
                    device_id={"step": after, "ctx": owner},
                    device_id_type=MESH,
                ).start()

        return 0

    lax.fori_loop(0, 3 * blocks, step, 0)

    @pl.when(clean)
    def _():
        got(early, q_sent.at[0])

    @pl.when(jnp.logical_not(clean))
    def _():
        got(early, k_sent.at[0])
        got(early, v_sent.at[0])

    @pl.when(jnp.logical_not(clean))
    def _():
        got(early, q_sent.at[0])

    for sent in (q_sent, k_sent, v_sent):
        got(late, sent.at[1])
    for which in range(2):
        got(others, c_sent.at[which])

        @pl.when(jnp.logical_and(clean, jnp.logical_not(own_holder)))
        def _():
            got(qh.at[pl.ds(0, rows)], first_sent.at[which])

    latent_copy.wait()
    got(mine, o_sent)
    got(gated_ref, o_got)


def body(latent, q, k, v, cache_keys, cache_values, time_weight, timestep, span_index, prefix_spans):
    rows, width = q.shape[1:]
    total = cache_keys.shape[0] // 2
    half = jnp.bfloat16
    smem = pl.BlockSpec(memory_space=pltpu.SMEM)
    hbm = pl.BlockSpec(memory_space=pl.ANY)
    dma = pltpu.SemaphoreType.DMA
    freqs = table()
    moved, gated = pl.pallas_call(
        kernel,
        out_shape=[jax.ShapeDtypeStruct((rows, width), half)] * 2,
        in_specs=[smem] * 3 + [hbm] * 8,
        out_specs=[hbm] * 2,
        scratch_shapes=[
            pltpu.VMEM(freqs.shape, jnp.float32),
            pltpu.VMEM((rows, width), half),
            pltpu.VMEM((rows, width), half),
            pltpu.VMEM((2 * total, 128), half),
            pltpu.VMEM((2 * total, 128), half),
            pltpu.VMEM((FREQS, 128), half),
            pltpu.VMEM((width // 128, rows, 128), half),
            pltpu.VMEM((width // 128, rows, 128), half),
            pltpu.VMEM((total, 128), half),
            pltpu.VMEM((total, 128), half),
            pltpu.VMEM((total, 128), half),
            pltpu.VMEM((total, 128), half),
            pltpu.VMEM((total, 128), half),
            pltpu.VMEM((total, 256), jnp.float32),
            pltpu.VMEM((total, 128), jnp.float32),
            pltpu.VMEM((1, 128), jnp.float32),
            pltpu.VMEM((total, 128), half),
            dma((6,)),
            dma((2,)),
            dma((2,)),
            dma((2,)),
            dma((total // BLOCK,)),
            dma((2,)),
            dma((2,)),
            dma((2,)),
            dma((2,)),
            dma((2,)),
            dma,
            dma,
            dma,
            dma,
            pltpu.SemaphoreType.REGULAR,
            pltpu.SemaphoreType.REGULAR,
        ],
        compiler_params=pltpu.CompilerParams(
            collective_id=0, has_side_effects=True, vmem_limit_bytes=56 * 1024 * 1024
        ),
    )(timestep, span_index, prefix_spans, jnp.asarray(freqs), latent[0], q[0], k[0], v[0], cache_keys, cache_values, time_weight)
    advanced = (moved.astype(jnp.float32) + gated.astype(jnp.float32)).astype(half)
    return advanced[None]


def solution(mesh):
    spans = P("step", "ctx", None)
    heads = P(None, "ctx")
    return jax.shard_map(
        body,
        mesh=mesh,
        in_specs=(spans,) * 4 + (heads,) * 3 + (P(),) * 3,
        out_specs=spans,
        check_vma=False,
    )
```
